512 devices in a mesh: seq: 16 (over x, z_lo), tensor: 32 (over z_hi, y, core).
Axes of the slice: x: 4, y: 8, z: 8 (z_hi: 2, z_lo: 4; z = z_hi * 4 + z_lo), core: 2. Of those that a mesh axis runs over, the one named last changes fastest.
Arguments:
- inputs: bfloat16 [3072, 8192], P(('seq', 'tensor')), may hold values from -6 to 6
- grad_out: bfloat16 [3072, 8192], P(('seq', 'tensor')), may hold values from -6 to 6
- up_blocks: bfloat16 [224, 8, 128, 128], P('tensor'), may hold values from -0.1875 to 0.1875
- up_index: int32 [224, 8], P('tensor'), may hold values from 0 to 63, as said below
- down_blocks: bfloat16 [224, 8, 128, 128], P('tensor'), may hold values from -0.1875 to 0.1875
- down_index: int32 [224, 8], P('tensor'), may hold values from 0 to 63, as said below
Outputs:
- grad_in: bfloat16 [3072, 8192], P(('seq', 'tensor'))
- grad_up: bfloat16 [224, 8, 128, 128], P('tensor', None, 'seq')
- grad_down: bfloat16 [224, 8, 128, 128], P('tensor', None, 'seq')
The draws below stay inside these ranges and needn't reach their ends.
Inputs may be any that keep to these rules, and one draw needn't show every extreme that they name: `up_index`: in every row the 8 block numbers are different, and every number from 0 to 63 appears in some row. `down_index`: in every row the 8 block numbers are different, and every number from 0 to 63 appears in some row.
All inputs are finite; a program needn't handle non-finite values.
Results may differ from the reference program's by a relative error of at most 0.012.
Values may be sent and summed in bfloat16 or wider, within the bound.
No kernel may reach another device: no remote copies, remote signals or barrier semaphores. Data moves between devices by JAX's collectives and lax.ppermute only.
A program may use at most 64 MiB of HBM per device.

```python
import math
import jax
import jax.numpy as jnp
from jax import lax

D = 8192
BS = 128
K = 8
TOK_SEQ = 192
NDB = 64
NBH = 224
TOKENS = 3072
N_SEQ = 16
N_TENSOR = 32


def mask_offsets():
    values = [0]
    power = 1
    while power < NDB:
        values.append(power)
        power = power * 2
    if NDB - 1 not in values:
        values.append(NDB - 1)
    for extra in range(NDB):
        if extra not in values:
            values.append(extra)
    return values[:K]


def butterfly_index(key):
    relabel = jax.random.permutation(jax.random.fold_in(key, 11), NDB).astype(jnp.int32)
    offset = jax.random.randint(jax.random.fold_in(key, 12), (), 0, NDB, dtype=jnp.int32)
    masks = jnp.array(mask_offsets(), dtype=jnp.int32)
    base = (jnp.arange(NBH, dtype=jnp.int32) + offset) % NDB
    return relabel[jnp.bitwise_xor(base[:, None], masks[None, :])]


def draw_up_index(key, part):
    key = jax.random.fold_in(key, 3)
    return butterfly_index(key)


def draw_down_index(key, part):
    key = jax.random.fold_in(key, 5)
    return butterfly_index(key)


def level_of(stream_key, dims, pieces, smallest, largest):
    loudness, own = 1.0, jax.random.fold_in(stream_key, 6)
    for position, shards_of in pieces:
        draws = jnp.exp(jax.random.uniform(jax.random.fold_in(own, position), (shards_of,), jnp.float32, smallest / len(pieces), largest / len(pieces)))
        loudness = loudness * jnp.repeat(draws, dims[position] // shards_of).reshape([-1 if axis == position else 1 for axis in range(len(dims))])
    return loudness


def gaussian(stream_key, extent, scale, reach, split=(), held_as=jnp.bfloat16):
    entries = scale * jax.random.normal(stream_key, extent, jnp.float32)
    if split:
        entries = entries * level_of(stream_key, extent, split, -0.22, 0.18)
    return jnp.clip(entries, -reach, reach).astype(held_as)


def setup_inputs(seed: int = 0) -> dict:
    seeds = jax.random.split(jax.random.key(seed), 7)
    return {
        "inputs": gaussian(seeds[0], (TOKENS, D), 1.0, 6.0, ((0, 512),)),
        "grad_out": gaussian(seeds[1], (TOKENS, D), 1.0, 6.0, ((0, 512),)),
        "up_blocks": gaussian(seeds[2], (NBH, K, BS, BS), (K * BS) ** -0.5, 0.1875, ((0, 32),)),
        "up_index": draw_up_index(jax.random.fold_in(seeds[6], 71), 0),
        "down_blocks": gaussian(seeds[4], (NBH, K, BS, BS), (K * BS) ** -0.5, 0.1875, ((0, 32),)),
        "down_index": draw_down_index(jax.random.fold_in(seeds[6], 71), 0),
    }


def reference(inputs, grad_out, up_blocks, up_index, down_blocks, down_index):
    blocks_wide = D // BS
    local_blocks = NBH // N_TENSOR
    factor = 1.0 / math.sqrt(TOKENS)
    grouped_in = inputs.reshape(N_SEQ, TOK_SEQ, blocks_wide, BS)
    grouped_grad = grad_out.reshape(N_SEQ, TOK_SEQ, blocks_wide, BS)

    def one_group(totals, stacked):
        up_now, up_where, down_now, down_where = stacked
        up_where = up_where.astype(jnp.int32)
        down_where = down_where.astype(jnp.int32)
        picked = jnp.take(grouped_in, up_where, axis=2).astype(jnp.float32)
        picked_grad = jnp.take(grouped_grad, down_where, axis=2).astype(jnp.float32)
        up_float = up_now.astype(jnp.float32)
        preact = jnp.einsum('srjkc,jkch->srjh', picked, up_float)
        hidden_grad = jnp.einsum('srjko,jkho->srjh', picked_grad, down_now.astype(jnp.float32))
        gating = jax.nn.sigmoid(preact)
        activated = (preact * gating).astype(jnp.bfloat16).astype(jnp.float32)
        preact_grad = (hidden_grad * gating * (1.0 + preact * (1.0 - gating))).astype(jnp.bfloat16).astype(jnp.float32)
        up_part = (jnp.einsum('srjkc,srjh->sjkch', picked, preact_grad) * factor).astype(jnp.bfloat16)
        down_part = (jnp.einsum('srjh,srjko->sjkho', activated, picked_grad) * factor).astype(jnp.bfloat16)
        grad_up = lax.optimization_barrier(jnp.sum(up_part.astype(jnp.float32), axis=0)).astype(jnp.bfloat16)
        grad_down = lax.optimization_barrier(jnp.sum(down_part.astype(jnp.float32), axis=0)).astype(jnp.bfloat16)
        contrib = jnp.einsum('srjh,jkch->srjkc', preact_grad, up_float)
        contrib = contrib.reshape(N_SEQ, TOK_SEQ, local_blocks * K, BS)
        partial_value = jnp.zeros((N_SEQ, TOK_SEQ, blocks_wide, BS), jnp.float32)
        partial_value = partial_value.at[:, :, up_where.reshape(-1)].add(contrib)
        partial_value = partial_value.astype(jnp.bfloat16).astype(jnp.float32)
        return (totals + partial_value, (grad_up, grad_down))
    stacked = (up_blocks.reshape(N_TENSOR, local_blocks, K, BS, BS), up_index.reshape(N_TENSOR, local_blocks, K), down_blocks.reshape(N_TENSOR, local_blocks, K, BS, BS), down_index.reshape(N_TENSOR, local_blocks, K))
    initial = jnp.zeros((N_SEQ, TOK_SEQ, blocks_wide, BS), jnp.float32)
    totals, grads = lax.scan(one_group, initial, stacked)
    grad_in = totals.astype(jnp.bfloat16).reshape(TOKENS, D)
    grad_up = grads[0].reshape(NBH, K, BS, BS)
    grad_down = grads[1].reshape(NBH, K, BS, BS)
    return (grad_in, grad_up, grad_down)
```

```python
import functools
import math

import jax
import jax.numpy as jnp
from jax import lax
from jax.experimental import pallas as pl
from jax.experimental.pallas import tpu as pltpu
from jax.sharding import PartitionSpec as P

Z_HI, Y, CORE = 2, 8, 2
X, Z_LO = 4, 4
VMEM_LIMIT = 40 * 1024 * 1024


def tensor_id(zh, y, c):
    return (zh * Y + y) * CORE + c


def tensor_pairs(move):
    return [
        (tensor_id(zh, y, c), tensor_id(*move(zh, y, c)))
        for zh in range(Z_HI)
        for y in range(Y)
        for c in range(CORE)
    ]


SIBLING = tensor_pairs(lambda zh, y, c: (zh, y, 1 - c))
Z_PARTNER = tensor_pairs(lambda zh, y, c: (1 - zh, y, c))
Y_UP = tensor_pairs(lambda zh, y, c: (zh, (y + 1) % Y, c))
Y_DOWN = tensor_pairs(lambda zh, y, c: (zh, (y - 1) % Y, c))
Y_GROUPS = [[tensor_id(zh, y, c) for y in range(Y)] for zh in range(Z_HI) for c in range(CORE)]
X_GROUPS = [[x * Z_LO + z for x in range(X)] for z in range(Z_LO)]
Z_GROUPS = [[x * Z_LO + z for z in range(Z_LO)] for x in range(X)]

NT = (((1,), (1,)), ((), ()))
TN = (((0,), (0,)), ((), ()))


def weight_kernel(factor, core_ref, upi_ref, downi_ref, mine_ref, other_ref, up_ref, down_ref,
                  parts_ref, pg_ref, x_ref, g_ref, xj_ref, gj_ref, wj_ref, sem):
    j = pl.program_id(0)
    slots = up_ref.shape[1]
    block = up_ref.shape[2]
    share = parts_ref.shape[4]

    @pl.when(j == 0)
    def _():
        @pl.when(core_ref[0] == 0)
        def _():
            first = pltpu.make_async_copy(mine_ref, x_ref, sem.at[0])
            second = pltpu.make_async_copy(other_ref, g_ref, sem.at[1])
            first.start()
            second.start()
            first.wait()
            second.wait()

        @pl.when(core_ref[0] != 0)
        def _():
            first = pltpu.make_async_copy(other_ref, x_ref, sem.at[0])
            second = pltpu.make_async_copy(mine_ref, g_ref, sem.at[1])
            first.start()
            second.start()
            first.wait()
            second.wait()

    for k in range(slots):
        here = pl.ds(k * block, block)
        at = pl.multiple_of(upi_ref[j, k] * block, block)
        xj_ref[:, here] = x_ref[:, pl.ds(at, block)]
        at = pl.multiple_of(downi_ref[j, k] * block, block)
        gj_ref[:, here] = g_ref[:, pl.ds(at, block)]
        wj_ref[:, here] = down_ref[0, k]
    xj = xj_ref[...]
    gj = gj_ref[...]
    preact = jnp.dot(xj, up_ref[0].reshape(slots * block, block), preferred_element_type=jnp.float32)
    hidden = lax.dot_general(gj, wj_ref[...], NT, preferred_element_type=jnp.float32)
    gating = jax.nn.sigmoid(preact)
    activated = (preact * gating).astype(jnp.bfloat16)
    pg = (hidden * gating * (1.0 + preact * (1.0 - gating))).astype(jnp.bfloat16)
    pg_ref[0] = pg
    up_sum = lax.dot_general(xj, pg, TN, preferred_element_type=jnp.float32)
    up_sum = (up_sum * factor).astype(jnp.bfloat16)
    down_sum = lax.dot_general(activated, gj, TN, preferred_element_type=jnp.float32)
    down_sum = (down_sum * factor).astype(jnp.bfloat16)
    for q in range(parts_ref.shape[0]):
        for k in range(slots):
            parts_ref[q, 0, 0, k] = up_sum[k * block + q * share:k * block + (q + 1) * share]
            parts_ref[q, 1, 0, k] = down_sum[q * share:(q + 1) * share, k * block:(k + 1) * block]


def input_kernel(core_ref, upi_ref, pg_ref, up_ref, keep_ref, send_ref, acc_ref):
    j = pl.program_id(0)
    slots = up_ref.shape[1]
    block = up_ref.shape[2]
    half = keep_ref.shape[1]

    @pl.when(j == 0)
    def _():
        acc_ref[...] = jnp.zeros_like(acc_ref)

    terms = lax.dot_general(pg_ref[0], up_ref[0].reshape(slots * block, block), NT,
                            preferred_element_type=jnp.float32)
    for k in range(slots):
        at = pl.multiple_of(upi_ref[j, k] * block, block)
        acc_ref[:, pl.ds(at, block)] += terms[:, k * block:(k + 1) * block]

    @pl.when(j == pl.num_programs(0) - 1)
    def _():
        own = pl.multiple_of(core_ref[0] * half, half)
        rest = pl.multiple_of((1 - core_ref[0]) * half, half)
        keep_ref[...] = acc_ref[:, pl.ds(own, half)].astype(jnp.bfloat16)
        send_ref[...] = acc_ref[:, pl.ds(rest, half)].astype(jnp.bfloat16)


def weight_parts(factor, core, up_index, down_index, mine, other, up_blocks, down_blocks):
    hidden, slots, block, _ = up_blocks.shape
    rows, features = mine.shape
    share = block // X
    whole = pl.BlockSpec((1, slots, block, block), lambda j, *_: (j, 0, 0, 0))
    flops = 4 * 2 * rows * hidden * slots * block * block
    return pl.pallas_call(
        functools.partial(weight_kernel, factor),
        grid_spec=pltpu.PrefetchScalarGridSpec(
            num_scalar_prefetch=3,
            grid=(hidden,),
            in_specs=[pl.BlockSpec(memory_space=pl.ANY), pl.BlockSpec(memory_space=pl.ANY), whole, whole],
            out_specs=[
                pl.BlockSpec((X, 2, 1, slots, share, block), lambda j, *_: (0, 0, j, 0, 0, 0)),
                pl.BlockSpec((1, rows, block), lambda j, *_: (j, 0, 0)),
            ],
            scratch_shapes=[
                pltpu.VMEM((rows, features), jnp.bfloat16),
                pltpu.VMEM((rows, features), jnp.bfloat16),
                pltpu.VMEM((rows, slots * block), jnp.bfloat16),
                pltpu.VMEM((rows, slots * block), jnp.bfloat16),
                pltpu.VMEM((block, slots * block), jnp.bfloat16),
                pltpu.SemaphoreType.DMA((2,)),
            ],
        ),
        out_shape=[
            jax.ShapeDtypeStruct((X, 2, hidden, slots, share, block), jnp.bfloat16),
            jax.ShapeDtypeStruct((hidden, rows, block), jnp.bfloat16),
        ],
        compiler_params=pltpu.CompilerParams(vmem_limit_bytes=VMEM_LIMIT),
        cost_estimate=pl.CostEstimate(flops=flops, bytes_accessed=14 * 2**20, transcendentals=0),
        name="weight_parts",
    )(core, up_index, down_index, mine, other, up_blocks, down_blocks)


def input_parts(core, up_index, pg, up_blocks, features):
    hidden, slots, block, _ = up_blocks.shape
    rows = pg.shape[1]
    half = features // 2
    flops = 2 * rows * hidden * slots * block * block
    out = pl.BlockSpec((rows, half), lambda j, *_: (0, 0))
    return pl.pallas_call(
        input_kernel,
        grid_spec=pltpu.PrefetchScalarGridSpec(
            num_scalar_prefetch=2,
            grid=(hidden,),
            in_specs=[
                pl.BlockSpec((1, rows, block), lambda j, *_: (j, 0, 0)),
                pl.BlockSpec((1, slots, block, block), lambda j, *_: (j, 0, 0, 0)),
            ],
            out_specs=[out, out],
            scratch_shapes=[pltpu.VMEM((rows, features), jnp.float32)],
        ),
        out_shape=[jax.ShapeDtypeStruct((rows, half), jnp.bfloat16)] * 2,
        compiler_params=pltpu.CompilerParams(vmem_limit_bytes=VMEM_LIMIT),
        cost_estimate=pl.CostEstimate(flops=flops, bytes_accessed=6 * 2**20, transcendentals=0),
        name="input_parts",
    )(core, up_index, pg, up_blocks)


def in_order(first_is_mine, mine, other):
    a = jnp.where(first_is_mine, mine, other)
    b = jnp.where(first_is_mine, other, mine)
    return jnp.concatenate([a, b], axis=0)


def add(a, b):
    return (a.astype(jnp.float32) + b.astype(jnp.float32)).astype(jnp.bfloat16)


def gather_rows(inputs, grad_out, core, y, z_hi):
    send = jnp.where(core == 0, grad_out, inputs)
    keep = jnp.where(core == 0, inputs, grad_out)
    pair = in_order(core == 0, keep, lax.ppermute(send, "tensor", SIBLING))
    chunk = in_order(z_hi == 0, pair, lax.ppermute(pair, "tensor", Z_PARTNER))
    rows, features = chunk.shape
    half = features // 2
    whole = jnp.zeros((Y, rows, features), chunk.dtype)

    def place(whole, piece, steps, column=0):
        return lax.dynamic_update_slice(whole, piece[None], ((y - steps) & (Y - 1), 0, column))

    whole = place(whole, chunk, 0)
    up = down = chunk
    for step in range(1, Y // 2):
        up = lax.ppermute(up, "tensor", Y_UP)
        down = lax.ppermute(down, "tensor", Y_DOWN)
        whole = place(whole, up, step)
        whole = place(whole, down, Y - step)
    last_up = lax.ppermute(up[:, :half], "tensor", Y_UP)
    last_down = lax.ppermute(down[:, half:], "tensor", Y_DOWN)
    whole = place(whole, last_up, Y // 2)
    whole = place(whole, last_down, Y // 2, half)
    return whole.reshape(Y * rows, features)


def reduce_weights(parts):
    _, kinds, hidden, slots, share, block = parts.shape
    units = kinds * hidden * slots
    part = lax.all_to_all(parts.reshape(X, units, share, block), "seq", 0, 0,
                          axis_index_groups=X_GROUPS, tiled=True)
    part = jnp.sum(part.astype(jnp.float32), axis=0).astype(jnp.bfloat16)
    part = part.reshape(units, Z_LO, share // Z_LO, block).transpose(1, 0, 2, 3)
    part = lax.all_to_all(part, "seq", 0, 0, axis_index_groups=Z_GROUPS, tiled=True)
    part = jnp.sum(part.astype(jnp.float32), axis=0).astype(jnp.bfloat16)
    part = part.reshape(kinds, hidden, slots, share // Z_LO, block)
    return part[0], part[1]


def reduce_inputs(keep, send, core, z_hi):
    part = add(keep, lax.ppermute(send, "tensor", SIBLING))
    part = lax.psum_scatter(part, "tensor", axis_index_groups=Y_GROUPS, tiled=True)
    rows = part.shape[0] // 2
    mine = lax.dynamic_slice_in_dim(part, z_hi * rows, rows)
    theirs = lax.dynamic_slice_in_dim(part, (1 - z_hi) * rows, rows)
    part = add(mine, lax.ppermute(theirs, "tensor", Z_PARTNER))
    rows = rows // 2
    mine = lax.dynamic_slice_in_dim(part, core * rows, rows)
    theirs = lax.dynamic_slice_in_dim(part, (1 - core) * rows, rows)
    other = lax.ppermute(theirs, "tensor", SIBLING)
    left = jnp.where(core == 0, mine, other)
    right = jnp.where(core == 0, other, mine)
    return jnp.concatenate([left, right], axis=1)


def local(inputs, grad_out, up_blocks, up_index, down_blocks, down_index):
    t = lax.axis_index("tensor")
    core = t & (CORE - 1)
    y = (t >> 1) & (Y - 1)
    z_hi = t >> 4
    rows_here, features = inputs.shape
    factor = 1.0 / math.sqrt(rows_here * lax.axis_size("tensor") * lax.axis_size("seq"))
    mine = gather_rows(inputs, grad_out, core, y, z_hi)
    other = lax.ppermute(mine, "tensor", SIBLING)
    core_arg = core.reshape(1).astype(jnp.int32)
    parts, pg = weight_parts(factor, core_arg, up_index, down_index, mine, other, up_blocks, down_blocks)
    keep, send = input_parts(core_arg, up_index, pg, up_blocks, features)
    grad_up, grad_down = reduce_weights(parts)
    grad_in = reduce_inputs(keep, send, core, z_hi)
    return (grad_in, grad_up, grad_down)


def solution(mesh):
    return jax.shard_map(
        local,
        mesh=mesh,
        in_specs=(
            P(("seq", "tensor"), None),
            P(("seq", "tensor"), None),
            P("tensor", None, None, None),
            P("tensor", None),
            P("tensor", None, None, None),
            P("tensor", None),
        ),
        out_specs=(
            P(("seq", "tensor"), None),
            P("tensor", None, "seq", None),
            P("tensor", None, "seq", None),
        ),
        check_vma=False,
    )
```

```python
import functools
import math

import jax
import jax.numpy as jnp
from jax import lax
from jax.experimental import pallas as pl
from jax.experimental.pallas import tpu as pltpu
from jax.sharding import PartitionSpec as P

Z_HI, Y, CORE = 2, 8, 2
X, Z_LO = 4, 4


def tensor_id(zh, y, c):
    return (zh * Y + y) * CORE + c


def tensor_pairs(move):
    return [
        (tensor_id(zh, y, c), tensor_id(*move(zh, y, c)))
        for zh in range(Z_HI)
        for y in range(Y)
        for c in range(CORE)
    ]


SIBLING = tensor_pairs(lambda zh, y, c: (zh, y, 1 - c))
Z_PARTNER = tensor_pairs(lambda zh, y, c: (1 - zh, y, c))
Y_UP = tensor_pairs(lambda zh, y, c: (zh, (y + 1) % Y, c))
Y_DOWN = tensor_pairs(lambda zh, y, c: (zh, (y - 1) % Y, c))
ROW_GROUPS = [[tensor_id(zh, y, c) for zh in range(Z_HI) for y in range(Y)] for c in range(CORE)]


def seq_pairs(dx, dz):
    return [(x * Z_LO + z, (x ^ dx) * Z_LO + (z ^ dz)) for x in range(X) for z in range(Z_LO)]


X_EVEN = seq_pairs(1, 0)
X_ODD = seq_pairs(3, 0)
Z_TRADE = [seq_pairs(0, r) for r in range(Z_LO)]

NT = (((1,), (1,)), ((), ()))


def columns(rows, index_ref, j, k, block):
    side_by_side = []
    for slot in (k, k + 1):
        at = pl.multiple_of(index_ref[j, slot] * block, block)
        side_by_side.append(rows[:, pl.ds(at, block)])
    return jnp.concatenate(side_by_side, axis=1)


def block_kernel(factor, place_ref, upi_ref, downi_ref, mine_hbm, other_hbm, up_hbm, down_hbm,
                 send_ref, keep_ref, up0, up1, up2, up3, down0, down1, down2, down3,
                 parts_ref, inputs, grads, acc_ref, up_ref, down_ref, pg_ref, act_ref, us_ref, ds_ref, sems, out_sem):
    hidden, slots, block, _ = up_ref.shape
    pieces, rows, quarter = keep_ref.shape
    share = up0.shape[2]
    outs = (up0, up1, up2, up3, down0, down1, down2, down3)

    def load_rows(first, second):
        pltpu.make_async_copy(first, inputs, sems.at[2, 0]).start()
        pltpu.make_async_copy(second, grads, sems.at[2, 1]).start()

    @pl.when(place_ref[0] == 0)
    def _():
        load_rows(mine_hbm, other_hbm)

    @pl.when(place_ref[0] != 0)
    def _():
        load_rows(other_hbm, mine_hbm)

    loads = []
    for j in range(hidden):
        for at, (far, near) in enumerate(((up_hbm, up_ref), (down_hbm, down_ref))):
            loads.append(pltpu.make_async_copy(far.at[j], near.at[j], sems.at[at, j]))
            loads[-1].start()
    acc_ref[...] = jnp.zeros_like(acc_ref)
    pltpu.make_async_copy(mine_hbm, inputs, sems.at[2, 0]).wait()
    pltpu.make_async_copy(other_hbm, grads, sems.at[2, 1]).wait()

    for j in range(hidden):
        loads[2 * j].wait()
        loads[2 * j + 1].wait()
        preact = hidden_grad = 0.0
        for k in range(0, slots, 2):
            weights = up_ref[j, k:k + 2].reshape(2 * block, block)
            preact = preact + jnp.dot(columns(inputs, upi_ref, j, k, block), weights,
                                      preferred_element_type=jnp.float32)
            weights = jnp.concatenate([down_ref[j, k], down_ref[j, k + 1]], axis=1)
            hidden_grad = hidden_grad + lax.dot_general(
                columns(grads, downi_ref, j, k, block), weights, NT, preferred_element_type=jnp.float32)
        gating = jax.nn.sigmoid(preact)
        act_ref[j] = (preact * gating).astype(jnp.bfloat16).T
        pg = (hidden_grad * gating * (1.0 + preact * (1.0 - gating))).astype(jnp.bfloat16)
        pg_ref[j] = pg.T
        for k in range(0, slots, 2):
            terms = lax.dot_general(pg, up_ref[j, k:k + 2].reshape(2 * block, block), NT,
                                    preferred_element_type=jnp.float32)
            for slot in (k, k + 1):
                at = pl.multiple_of(upi_ref[j, slot] * block, block)
                acc_ref[:, pl.ds(at, block)] += terms[:, (slot - k) * block:(slot - k + 1) * block]

    @pl.loop(0, hidden)
    def _(j):
        pg = pg_ref[j]
        act = act_ref[j]
        for k in range(0, slots, 2):
            sums = jnp.dot(pg, columns(inputs, upi_ref, j, k, block), preferred_element_type=jnp.float32)
            sums = sums * factor
            for slot in (k, k + 1):
                us_ref[slot] = sums[:, (slot - k) * block:(slot - k + 1) * block].T
            sums = jnp.dot(act, columns(grads, downi_ref, j, k, block), preferred_element_type=jnp.float32)
            sums = sums * factor
            for slot in (k, k + 1):
                ds_ref[slot] = sums[:, (slot - k) * block:(slot - k + 1) * block]
        for q in range(X):
            row = pl.multiple_of((place_ref[1] ^ q) * share, share)
            parts_ref[q, j] = us_ref[:, pl.ds(row, share), :].astype(jnp.bfloat16)
            parts_ref[X + q, j] = ds_ref[:, pl.ds(row, share), :].astype(jnp.bfloat16)

    stores = [pltpu.make_async_copy(parts_ref.at[n], out, out_sem.at[n]) for n, out in enumerate(outs)]
    for store in stores:
        store.start()

    z_hi = place_ref[4]
    for out, core in ((send_ref, 1 - place_ref[0]), (keep_ref, place_ref[0])):
        left = pl.multiple_of(core * 2 * quarter, quarter)
        right = pl.multiple_of(core * 2 * quarter + quarter, quarter)
        for k in range(Y):
            owner = (place_ref[3] - k) & (Y - 1)
            here = slice(k * rows, (k + 1) * rows)
            a = acc_ref[here, pl.ds(left, quarter)]
            b = acc_ref[here, pl.ds(right, quarter)]
            half = rows // 2
            out[z_hi * Y + owner] = jnp.concatenate([a[:half], b[:half]], axis=0).astype(jnp.bfloat16)
            out[(1 - z_hi) * Y + owner] = jnp.concatenate([a[half:], b[half:]], axis=0).astype(jnp.bfloat16)
    for store in stores:
        store.wait()


def x_sum_kernel(place_ref, up_own, up_a, up_b, down_own, down_a, down_b, *refs):
    outs, sum_ref = refs[:Z_LO], refs[Z_LO]
    _, slots, share, block = up_own.shape
    rows = share // Z_LO
    for kind, parts in enumerate(((up_own, up_a, up_b), (down_own, down_a, down_b))):
        total = sum(part[0].astype(jnp.float32) for part in parts)
        sum_ref[kind] = total.reshape(slots * share, block)
        for r, out in enumerate(outs):
            row = pl.multiple_of((place_ref[2] ^ r) * rows, rows)
            piece = [sum_ref[kind, pl.ds(k * share + row, rows), :] for k in range(slots)]
            out[kind, 0] = jnp.concatenate(piece, axis=0).astype(jnp.bfloat16)


def add_kernel(a_ref, b_ref, out_ref):
    out_ref[...] = (a_ref[...].astype(jnp.float32) + b_ref[...].astype(jnp.float32)).astype(jnp.bfloat16)


def total_kernel(parts_ref, out_ref):
    total = sum(parts_ref[n].astype(jnp.float32) for n in range(parts_ref.shape[0]))
    out_ref[...] = total.astype(jnp.bfloat16)


SMEM = pl.BlockSpec(memory_space=pltpu.SMEM)
VMEM = pl.BlockSpec(memory_space=pltpu.VMEM)
HBM = pl.BlockSpec(memory_space=pltpu.HBM)


def block_parts(factor, place, up_index, down_index, mine, other, up_blocks, down_blocks):
    hidden, slots, block, _ = up_blocks.shape
    rows, features = mine.shape
    flops = 5 * 2 * rows * hidden * slots * block * block
    terms = jax.ShapeDtypeStruct((Z_HI * Y, rows // Y, features // 4), jnp.bfloat16)
    part = jax.ShapeDtypeStruct((hidden, slots, block // X, block), jnp.bfloat16)
    return pl.pallas_call(
        functools.partial(block_kernel, factor),
        in_specs=[SMEM] * 3 + [pl.BlockSpec(memory_space=pl.ANY)] * 2 + [HBM] * 2,
        out_specs=[VMEM] * 2 + [HBM] * 8,
        out_shape=[terms] * 2 + [part] * 8,
        scratch_shapes=[
            pltpu.VMEM((2 * X,) + part.shape, jnp.bfloat16),
            pltpu.VMEM((rows, features), jnp.bfloat16),
            pltpu.VMEM((rows, features), jnp.bfloat16),
            pltpu.VMEM((rows, features), jnp.float32),
            pltpu.VMEM(up_blocks.shape, jnp.bfloat16),
            pltpu.VMEM(down_blocks.shape, jnp.bfloat16),
            pltpu.VMEM((hidden, block, rows), jnp.bfloat16),
            pltpu.VMEM((hidden, block, rows), jnp.bfloat16),
            pltpu.VMEM((slots, block, block), jnp.float32),
            pltpu.VMEM((slots, block, block), jnp.float32),
            pltpu.SemaphoreType.DMA((3, hidden)),
            pltpu.SemaphoreType.DMA((2 * X,)),
        ],
        compiler_params=pltpu.CompilerParams(vmem_limit_bytes=52 * 2**20),
        cost_estimate=pl.CostEstimate(flops=flops, bytes_accessed=16 * 2**20, transcendentals=0),
        name="block_parts",
    )(place, up_index, down_index, mine, other, up_blocks, down_blocks)


def x_sum(place, *parts):
    hidden, slots, share, block = parts[0].shape
    rows = slots * share // Z_LO
    part = pl.BlockSpec((1, slots, share, block), lambda j, *_: (j, 0, 0, 0))
    return pl.pallas_call(
        x_sum_kernel,
        grid_spec=pltpu.PrefetchScalarGridSpec(
            num_scalar_prefetch=1,
            grid=(hidden,),
            in_specs=[part] * 6,
            out_specs=[pl.BlockSpec((2, 1, rows, block), lambda j, *_: (0, j, 0, 0))] * Z_LO,
            scratch_shapes=[pltpu.VMEM((2, slots * share, block), jnp.float32)],
        ),
        out_shape=[jax.ShapeDtypeStruct((2, hidden, rows, block), jnp.bfloat16)] * Z_LO,
        compiler_params=pltpu.CompilerParams(vmem_limit_bytes=8 * 2**20),
        cost_estimate=pl.CostEstimate(flops=2**21, bytes_accessed=4 * 2**20, transcendentals=0),
        name="x_sum",
    )(place, *parts)


def cost(microseconds):
    return pl.CostEstimate(flops=microseconds * 10**9, bytes_accessed=2**20, transcendentals=0)


SMALL = pltpu.CompilerParams(vmem_limit_bytes=6 * 2**20)


def add_terms(a, b, microseconds, name):
    half = a.shape[0] // 2 if a.shape[0] % 2 == 0 else a.shape[0]
    spec = pl.BlockSpec((half,) + a.shape[1:], lambda i: (i,) + (0,) * (a.ndim - 1))
    return pl.pallas_call(
        add_kernel, grid=(a.shape[0] // half,), in_specs=[spec] * 2, out_specs=spec,
        out_shape=jax.ShapeDtypeStruct(a.shape, jnp.bfloat16), cost_estimate=cost(microseconds), name=name,
        compiler_params=SMALL,
    )(a, b)


def total_terms(parts):
    pieces, rows, width = parts.shape
    share = width // 4
    return pl.pallas_call(
        total_kernel, grid=(4,),
        in_specs=[pl.BlockSpec((pieces, rows, share), lambda i: (0, 0, i))],
        out_specs=pl.BlockSpec((rows, share), lambda i: (0, i)),
        out_shape=jax.ShapeDtypeStruct((rows, width), jnp.bfloat16), cost_estimate=cost(30), name="total_terms", compiler_params=SMALL,
    )(parts)


def in_order(first_is_mine, mine, other):
    a = jnp.where(first_is_mine, mine, other)
    b = jnp.where(first_is_mine, other, mine)
    return jnp.concatenate([a, b], axis=0)


def gather_rows(inputs, grad_out, core, zero):
    send = jnp.where(core == 0, grad_out, inputs)
    keep = jnp.where(core == 0, inputs, grad_out)
    pair = in_order(core == 0, keep, lax.ppermute(send, "tensor", SIBLING))
    rows, features = pair.shape
    half = features // 2
    pair = jnp.concatenate([pair[:, :half], pair[:, half:]], axis=0)
    other = lax.ppermute(pair, "tensor", Z_PARTNER)
    left = jnp.concatenate([pair[:rows], other[:rows]], axis=0)
    right = jnp.concatenate([pair[rows:], other[rows:]], axis=0)
    chunk = jnp.concatenate([left, right], axis=1)
    whole = jnp.zeros((Y, 2 * rows, features), chunk.dtype)

    def place(whole, piece, at, column=0):
        return lax.dynamic_update_slice(whole, piece[None], (zero + at, 0, column))

    whole = place(whole, chunk, 0)
    up = down = chunk
    for step in range(1, Y // 2):
        up = lax.ppermute(up, "tensor", Y_UP)
        down = lax.ppermute(down, "tensor", Y_DOWN)
        whole = place(place(whole, up, step), down, Y - step)
    whole = place(whole, lax.ppermute(up[:, :half], "tensor", Y_UP), Y // 2)
    whole = place(whole, lax.ppermute(down[:, half:], "tensor", Y_DOWN), Y // 2, half)
    return whole.reshape(-1, features)


def reduce_weights_x(place, up, down):
    far_up = lax.ppermute(up[2], "seq", X_EVEN)
    far_down = lax.ppermute(down[2], "seq", X_ODD)
    up_a = lax.ppermute(up[1], "seq", X_EVEN)
    down_b = lax.ppermute(down[3], "seq", X_ODD)
    up_b = lax.ppermute(add_terms(up[3], far_up, 20, "add_up"), "seq", X_ODD)
    down_a = lax.ppermute(add_terms(down[1], far_down, 20, "add_down"), "seq", X_EVEN)
    return x_sum(place, up[0], up_a, up_b, down[0], down_a, down_b)


def reduce_inputs(keep, send):
    part = add_terms(keep, lax.ppermute(send, "tensor", SIBLING), 15, "add_cores")
    return lax.all_to_all(part, "tensor", 0, 0, axis_index_groups=ROW_GROUPS, tiled=True)


def own_rows(part, core):
    part = total_terms(part)
    rows = part.shape[0] // 4
    pair = jnp.concatenate([part[:2 * rows], part[2 * rows:]], axis=1)
    mine = jnp.where(core == 0, pair[:rows], pair[rows:])
    other = lax.ppermute(jnp.where(core == 0, pair[rows:], pair[:rows]), "tensor", SIBLING)
    left = jnp.where(core == 0, mine, other)
    right = jnp.where(core == 0, other, mine)
    return jnp.concatenate([left, right], axis=1)


def local(inputs, grad_out, up_blocks, up_index, down_blocks, down_index):
    t = lax.axis_index("tensor")
    core = t & (CORE - 1)
    z_hi = t >> 4
    rows_here, _ = inputs.shape
    factor = 1.0 / math.sqrt(rows_here * lax.axis_size("tensor") * lax.axis_size("seq"))
    mine = gather_rows(inputs, grad_out, core, t >> 5)
    other = lax.ppermute(mine, "tensor", SIBLING)
    seq = lax.axis_index("seq")
    y = (t >> 1) & (Y - 1)
    place = jnp.stack([core, seq >> 2, seq & (Z_LO - 1), y, z_hi]).astype(jnp.int32)
    send, keep, *parts = block_parts(factor, place, up_index, down_index, mine, other, up_blocks, down_blocks)
    hidden, slots, block, _ = up_blocks.shape
    shape = (hidden, slots, block // (X * Z_LO), block)
    input_terms = reduce_inputs(keep, send)
    pieces = reduce_weights_x(place, parts[:4], parts[4:])
    first = pieces[0]
    input_terms, first = lax.optimization_barrier((input_terms, first))
    grad_in = own_rows(input_terms, core)
    pieces = [first] + [lax.ppermute(pieces[r], "seq", Z_TRADE[r]) for r in (2, 3, 1)]
    total = sum(piece.astype(jnp.float32) for piece in pieces).astype(jnp.bfloat16)
    grad_up, grad_down = total[0].reshape(shape), total[1].reshape(shape)
    return (grad_in, grad_up, grad_down)


def solution(mesh):
    return jax.shard_map(
        local,
        mesh=mesh,
        in_specs=(
            P(("seq", "tensor"), None),
            P(("seq", "tensor"), None),
            P("tensor", None, None, None),
            P("tensor", None),
            P("tensor", None, None, None),
            P("tensor", None),
        ),
        out_specs=(
            P(("seq", "tensor"), None),
            P("tensor", None, "seq", None),
            P("tensor", None, "seq", None),
        ),
        check_vma=False,
    )
```

```python
import functools
import math

import jax
import jax.numpy as jnp
from jax import lax
from jax.experimental import pallas as pl
from jax.experimental.pallas import tpu as pltpu
from jax.sharding import PartitionSpec as P

Z_HI, Y, CORE = 2, 8, 2
X, Z_LO = 4, 4


def tensor_id(zh, y, c):
    return (zh * Y + y) * CORE + c


def tensor_pairs(move):
    return [
        (tensor_id(zh, y, c), tensor_id(*move(zh, y, c)))
        for zh in range(Z_HI)
        for y in range(Y)
        for c in range(CORE)
    ]


SIBLING = tensor_pairs(lambda zh, y, c: (zh, y, 1 - c))
Z_PARTNER = tensor_pairs(lambda zh, y, c: (1 - zh, y, c))
Y_UP = tensor_pairs(lambda zh, y, c: (zh, (y + 1) % Y, c))
Y_DOWN = tensor_pairs(lambda zh, y, c: (zh, (y - 1) % Y, c))
ROW_GROUPS = [[tensor_id(zh, y, c) for zh in range(Z_HI) for y in range(Y)] for c in range(CORE)]


def seq_pairs(dx, dz):
    return [(x * Z_LO + z, (x ^ dx) * Z_LO + (z ^ dz)) for x in range(X) for z in range(Z_LO)]


X_EVEN = seq_pairs(1, 0)
X_ODD = seq_pairs(3, 0)
Z_TRADE = [seq_pairs(0, r) for r in range(Z_LO)]

NT = (((1,), (1,)), ((), ()))


UP_PLACE = (4, 1, 0, 5)
DOWN_PLACE = (6, 7, 2, 3)


def columns(rows, index_ref, j, k, block):
    side_by_side = []
    for slot in (k, k + 1):
        at = pl.multiple_of(index_ref[j, slot] * block, block)
        side_by_side.append(rows[:, pl.ds(at, block)])
    return jnp.concatenate(side_by_side, axis=1)


def block_kernel(factor, place_ref, upi_ref, downi_ref, mine_a, mine_b, other_a, other_b, up_hbm, down_hbm,
                 send_ref, keep_ref, even_out, odd_out, up0, up3, down0, down1,
                 parts_ref, inputs, grads, acc_ref, up_ref, down_ref, pre_ref, pg_ref, act_ref, us_ref, ds_ref, sems, out_sem):
    hidden, slots, block, _ = up_ref.shape
    pieces, rows, quarter = keep_ref.shape
    share = up0.shape[2]

    split = mine_a.shape[0]

    def row_copies(parts, into, at):
        return [pltpu.make_async_copy(parts[0], into.at[0:split], sems.at[at, 0]),
                pltpu.make_async_copy(parts[1], into.at[split:], sems.at[at, 1])]

    def start_rows(into, at, wanted):
        @pl.when(place_ref[0] == wanted)
        def _():
            for load in row_copies((mine_a, mine_b), into, at):
                load.start()

        @pl.when(place_ref[0] != wanted)
        def _():
            for load in row_copies((other_a, other_b), into, at):
                load.start()

    start_rows(inputs, 2, 0)
    up_loads = [pltpu.make_async_copy(up_hbm.at[j], up_ref.at[j], sems.at[0, j]) for j in range(hidden)]
    down_loads = [pltpu.make_async_copy(down_hbm.at[j], down_ref.at[j], sems.at[1, j]) for j in range(hidden)]
    for load in up_loads:
        load.start()
    start_rows(grads, 3, 1)
    for load in down_loads:
        load.start()
    acc_ref[...] = jnp.zeros_like(acc_ref)
    for load in row_copies((mine_a, mine_b), inputs, 2):
        load.wait()
    for j in range(hidden):
        up_loads[j].wait()
        preact = 0.0
        for k in range(0, slots, 2):
            weights = up_ref[j, k:k + 2].reshape(2 * block, block)
            preact = preact + jnp.dot(columns(inputs, upi_ref, j, k, block), weights,
                                      preferred_element_type=jnp.float32)
        pre_ref[j] = preact
    for load in row_copies((mine_a, mine_b), grads, 3):
        load.wait()

    for j in range(hidden):
        down_loads[j].wait()
        preact, hidden_grad = pre_ref[j], 0.0
        for k in range(0, slots, 2):
            weights = jnp.concatenate([down_ref[j, k], down_ref[j, k + 1]], axis=1)
            hidden_grad = hidden_grad + lax.dot_general(
                columns(grads, downi_ref, j, k, block), weights, NT, preferred_element_type=jnp.float32)
        gating = jax.nn.sigmoid(preact)
        act_ref[j] = (preact * gating).astype(jnp.bfloat16).T
        pg = (hidden_grad * gating * (1.0 + preact * (1.0 - gating))).astype(jnp.bfloat16)
        pg_ref[j] = pg.T
        for k in range(0, slots, 2):
            terms = lax.dot_general(pg, up_ref[j, k:k + 2].reshape(2 * block, block), NT,
                                    preferred_element_type=jnp.float32)
            for slot in (k, k + 1):
                at = pl.multiple_of(upi_ref[j, slot] * block, block)
                acc_ref[:, pl.ds(at, block)] += terms[:, (slot - k) * block:(slot - k + 1) * block]

    @pl.loop(0, hidden)
    def _(j):
        pg = pg_ref[j]
        act = act_ref[j]
        for k in range(0, slots, 2):
            sums = jnp.dot(pg, columns(inputs, upi_ref, j, k, block), preferred_element_type=jnp.float32)
            sums = (sums * factor).astype(jnp.bfloat16)
            for slot in (k, k + 1):
                us_ref[slot] = sums[:, (slot - k) * block:(slot - k + 1) * block].T
            sums = jnp.dot(act, columns(grads, downi_ref, j, k, block), preferred_element_type=jnp.float32)
            sums = (sums * factor).astype(jnp.bfloat16)
            for slot in (k, k + 1):
                ds_ref[slot] = sums[:, (slot - k) * block:(slot - k + 1) * block]
        for q in range(X):
            row = pl.multiple_of((place_ref[1] ^ q) * share, share)
            parts_ref[UP_PLACE[q], j] = us_ref[:, pl.ds(row, share), :]
            parts_ref[DOWN_PLACE[q], j] = ds_ref[:, pl.ds(row, share), :]

    pairs = [(parts_ref.at[0:2], even_out), (parts_ref.at[2:4], odd_out)]
    pairs += [(parts_ref.at[4 + n], out) for n, out in enumerate((up0, up3, down0, down1))]
    stores = [pltpu.make_async_copy(*pair, out_sem.at[n]) for n, pair in enumerate(pairs)]
    for store in stores:
        store.start()

    z_hi = place_ref[4]
    for out, core in ((send_ref, 1 - place_ref[0]), (keep_ref, place_ref[0])):
        left = pl.multiple_of(core * 2 * quarter, quarter)
        right = pl.multiple_of(core * 2 * quarter + quarter, quarter)
        for at, k in enumerate(FIRST + SECOND):
            owner = (place_ref[3] - k) & (Y - 1)
            here = slice(at * rows, (at + 1) * rows)
            a = acc_ref[here, pl.ds(left, quarter)]
            b = acc_ref[here, pl.ds(right, quarter)]
            half = rows // 2
            out[z_hi * Y + owner] = jnp.concatenate([a[:half], b[:half]], axis=0).astype(jnp.bfloat16)
            out[(1 - z_hi) * Y + owner] = jnp.concatenate([a[half:], b[half:]], axis=0).astype(jnp.bfloat16)
    for store in stores:
        store.wait()


def x_sum_kernel(place_ref, up_own, up_a, up_b, down_own, down_a, down_b, *refs):
    outs, sum_ref = refs[:Z_LO], refs[Z_LO]
    hidden, slots, share, block = up_own.shape
    rows = share // Z_LO
    for kind, parts in enumerate(((up_own, up_a.at[1], up_b), (down_own, down_a, down_b.at[1]))):
        for j in range(hidden):
            total = sum(part[j].astype(jnp.float32) for part in parts)
            sum_ref[kind, j] = total.reshape(slots * share, block)
            for r, out in enumerate(outs):
                row = pl.multiple_of((place_ref[2] ^ r) * rows, rows)
                piece = [sum_ref[kind, j, pl.ds(k * share + row, rows), :] for k in range(slots)]
                out[kind, j] = jnp.concatenate(piece, axis=0).astype(jnp.bfloat16)


def add_kernel(a_ref, b_ref, out_ref):
    out_ref[...] = (a_ref[...].astype(jnp.float32) + b_ref[...].astype(jnp.float32)).astype(jnp.bfloat16)


def total_kernel(parts_ref, out_ref):
    total = sum(parts_ref[n].astype(jnp.float32) for n in range(parts_ref.shape[0]))
    out_ref[...] = total.astype(jnp.bfloat16)


SMEM = pl.BlockSpec(memory_space=pltpu.SMEM)
VMEM = pl.BlockSpec(memory_space=pltpu.VMEM)
HBM = pl.BlockSpec(memory_space=pltpu.HBM)


def block_parts(factor, place, up_index, down_index, gathered, up_blocks, down_blocks):
    hidden, slots, block, _ = up_blocks.shape
    rows = gathered[0].shape[0] + gathered[1].shape[0]
    features = gathered[0].shape[1]
    flops = 5 * 2 * rows * hidden * slots * block * block
    terms = jax.ShapeDtypeStruct((Z_HI * Y, rows // Y, features // 4), jnp.bfloat16)
    part = jax.ShapeDtypeStruct((hidden, slots, block // X, block), jnp.bfloat16)
    both = jax.ShapeDtypeStruct((2,) + part.shape, jnp.bfloat16)
    return pl.pallas_call(
        functools.partial(block_kernel, factor),
        in_specs=[SMEM] * 3 + [HBM] * 6,
        out_specs=[VMEM] * 2 + [HBM] * 6,
        out_shape=[terms] * 2 + [both] * 2 + [part] * 4,
        scratch_shapes=[
            pltpu.VMEM((2 * X,) + part.shape, jnp.bfloat16),
            pltpu.VMEM((rows, features), jnp.bfloat16),
            pltpu.VMEM((rows, features), jnp.bfloat16),
            pltpu.VMEM((rows, features), jnp.float32),
            pltpu.VMEM(up_blocks.shape, jnp.bfloat16),
            pltpu.VMEM(down_blocks.shape, jnp.bfloat16),
            pltpu.VMEM((hidden, rows, block), jnp.float32),
            pltpu.VMEM((hidden, block, rows), jnp.bfloat16),
            pltpu.VMEM((hidden, block, rows), jnp.bfloat16),
            pltpu.VMEM((slots, block, block), jnp.bfloat16),
            pltpu.VMEM((slots, block, block), jnp.bfloat16),
            pltpu.SemaphoreType.DMA((4, hidden)),
            pltpu.SemaphoreType.DMA((2 * X,)),
        ],
        compiler_params=pltpu.CompilerParams(vmem_limit_bytes=58 * 2**20),
        cost_estimate=pl.CostEstimate(flops=flops, bytes_accessed=16 * 2**20, transcendentals=0),
        name="block_parts",
    )(place, up_index, down_index, *gathered, up_blocks, down_blocks)


def x_sum(place, *parts):
    hidden, slots, share, block = parts[0].shape
    rows = slots * share // Z_LO
    return pl.pallas_call(
        x_sum_kernel,
        in_specs=[SMEM] + [VMEM] * 6,
        out_specs=[VMEM] * Z_LO,
        out_shape=[jax.ShapeDtypeStruct((2, hidden, rows, block), jnp.bfloat16)] * Z_LO,
        scratch_shapes=[pltpu.VMEM((2, hidden, slots * share, block), jnp.float32)],
        compiler_params=pltpu.CompilerParams(vmem_limit_bytes=8 * 2**20),
        cost_estimate=pl.CostEstimate(flops=2**21, bytes_accessed=4 * 2**20, transcendentals=0),
        name="x_sum",
    )(place, *parts)


def cost(microseconds):
    return pl.CostEstimate(flops=microseconds * 10**9, bytes_accessed=2**20, transcendentals=0)


SMALL = pltpu.CompilerParams(vmem_limit_bytes=6 * 2**20)


def add_terms(a, b, microseconds, name):
    half = a.shape[0] // 2 if a.shape[0] % 2 == 0 else a.shape[0]
    rest = (0,) * (a.ndim - 1)
    spec = pl.BlockSpec((half,) + a.shape[1:], lambda i: (i,) + rest)
    first = pl.BlockSpec((None, half) + a.shape[1:], lambda i: (0, i) + rest)
    return pl.pallas_call(
        add_kernel, grid=(a.shape[0] // half,), in_specs=[spec, first if b.ndim > a.ndim else spec], out_specs=spec,
        out_shape=jax.ShapeDtypeStruct(a.shape, jnp.bfloat16), cost_estimate=cost(microseconds), name=name,
        compiler_params=SMALL,
    )(a, b)


def total_terms(parts):
    pieces, rows, width = parts.shape
    share = width // 4
    return pl.pallas_call(
        total_kernel, grid=(4,),
        in_specs=[pl.BlockSpec((pieces, rows, share), lambda i: (0, 0, i))],
        out_specs=pl.BlockSpec((rows, share), lambda i: (0, i)),
        out_shape=jax.ShapeDtypeStruct((rows, width), jnp.bfloat16), cost_estimate=cost(30), name="total_terms", compiler_params=SMALL,
    )(parts)


def in_order(first_is_mine, mine, other):
    a = jnp.where(first_is_mine, mine, other)
    b = jnp.where(first_is_mine, other, mine)
    return jnp.concatenate([a, b], axis=0)


FIRST = (0, 1, 7, 2, 6, 3)
SECOND = (5, 4)


def gather_rows(inputs, grad_out, core, zero):
    send = jnp.where(core == 0, grad_out, inputs)
    keep = jnp.where(core == 0, inputs, grad_out)
    pair = in_order(core == 0, keep, lax.ppermute(send, "tensor", SIBLING))
    rows, features = pair.shape
    half = features // 2
    pair = jnp.concatenate([pair[:, :half], pair[:, half:]], axis=0)
    other = lax.ppermute(pair, "tensor", Z_PARTNER)
    left = jnp.concatenate([pair[:rows], other[:rows]], axis=0)
    right = jnp.concatenate([pair[rows:], other[rows:]], axis=0)
    chunk = lax.optimization_barrier(jnp.concatenate([left, right], axis=1))
    first = jnp.zeros((len(FIRST), 2 * rows, features), chunk.dtype)
    second = jnp.zeros((len(SECOND), 2 * rows, features), chunk.dtype)

    def place(whole, piece, at, column=0):
        return lax.dynamic_update_slice(whole, piece[None], (zero + at, 0, column))

    first = place(first, chunk, FIRST.index(0))
    up = down = chunk
    for step in range(1, Y // 2):
        up = lax.ppermute(up, "tensor", Y_UP)
        down = lax.ppermute(down, "tensor", Y_DOWN)
        first = place(first, up, FIRST.index(step))
        if Y - step in FIRST:
            first = place(first, down, FIRST.index(Y - step))
    second = place(second, down, SECOND.index(Y // 2 + 1))
    second = place(second, lax.ppermute(up[:, :half], "tensor", Y_UP), SECOND.index(Y // 2))
    second = place(second, lax.ppermute(down[:, half:], "tensor", Y_DOWN), SECOND.index(Y // 2), half)
    return first.reshape(-1, features), second.reshape(-1, features)


def reduce_weights_x(place, even, odd, up_own, up_odd, down_own, down_even):
    even = lax.ppermute(even, "seq", X_EVEN)
    odd = lax.ppermute(odd, "seq", X_ODD)
    up_odd = lax.ppermute(add_terms(up_odd, even, 20, "add_up"), "seq", X_ODD)
    down_even = lax.ppermute(add_terms(down_even, odd, 20, "add_down"), "seq", X_EVEN)
    return x_sum(place, up_own, even, up_odd, down_own, down_even, odd)


def reduce_inputs(keep, send):
    part = add_terms(keep, lax.ppermute(send, "tensor", SIBLING), 15, "add_cores")
    return lax.all_to_all(part, "tensor", 0, 0, axis_index_groups=ROW_GROUPS, tiled=True)


def own_rows(part, core):
    part = total_terms(part)
    rows = part.shape[0] // 4
    pair = jnp.concatenate([part[:2 * rows], part[2 * rows:]], axis=1)
    mine = jnp.where(core == 0, pair[:rows], pair[rows:])
    other = lax.ppermute(jnp.where(core == 0, pair[rows:], pair[:rows]), "tensor", SIBLING)
    left = jnp.where(core == 0, mine, other)
    right = jnp.where(core == 0, other, mine)
    return jnp.concatenate([left, right], axis=1)


def local(inputs, grad_out, up_blocks, up_index, down_blocks, down_index):
    t = lax.axis_index("tensor")
    core = t & (CORE - 1)
    z_hi = t >> 4
    rows_here, _ = inputs.shape
    factor = 1.0 / math.sqrt(rows_here * lax.axis_size("tensor") * lax.axis_size("seq"))
    first, second = gather_rows(inputs, grad_out, core, t >> 5)
    gathered = (first, second, lax.ppermute(first, "tensor", SIBLING), lax.ppermute(second, "tensor", SIBLING))
    seq = lax.axis_index("seq")
    y = (t >> 1) & (Y - 1)
    place = jnp.stack([core, seq >> 2, seq & (Z_LO - 1), y, z_hi]).astype(jnp.int32)
    send, keep, *parts = block_parts(factor, place, up_index, down_index, gathered, up_blocks, down_blocks)
    hidden, slots, block, _ = up_blocks.shape
    shape = (hidden, slots, block // (X * Z_LO), block)
    input_terms = reduce_inputs(keep, send)
    pieces = reduce_weights_x(place, *parts)
    first = pieces[0]
    input_terms, first = lax.optimization_barrier((input_terms, first))
    grad_in = own_rows(input_terms, core)
    pieces = [first] + [lax.ppermute(pieces[r], "seq", Z_TRADE[r]) for r in (2, 3, 1)]
    total = sum(piece.astype(jnp.float32) for piece in pieces).astype(jnp.bfloat16)
    grad_up, grad_down = total[0].reshape(shape), total[1].reshape(shape)
    return (grad_in, grad_up, grad_down)


def solution(mesh):
    return jax.shard_map(
        local,
        mesh=mesh,
        in_specs=(
            P(("seq", "tensor"), None),
            P(("seq", "tensor"), None),
            P("tensor", None, None, None),
            P("tensor", None),
            P("tensor", None, None, None),
            P("tensor", None),
        ),
        out_specs=(
            P(("seq", "tensor"), None),
            P("tensor", None, "seq", None),
            P("tensor", None, "seq", None),
        ),
        check_vma=False,
    )
```

```python
import functools
import math

import jax
import jax.numpy as jnp
from jax import lax
from jax.experimental import pallas as pl
from jax.experimental.pallas import tpu as pltpu
from jax.sharding import PartitionSpec as P

Z_HI, Y, CORE = 2, 8, 2
X, Z_LO = 4, 4


def tensor_id(zh, y, c):
    return (zh * Y + y) * CORE + c


def tensor_pairs(move):
    return [
        (tensor_id(zh, y, c), tensor_id(*move(zh, y, c)))
        for zh in range(Z_HI)
        for y in range(Y)
        for c in range(CORE)
    ]


SIBLING = tensor_pairs(lambda zh, y, c: (zh, y, 1 - c))
Z_PARTNER = tensor_pairs(lambda zh, y, c: (1 - zh, y, c))
Y_UP = tensor_pairs(lambda zh, y, c: (zh, (y + 1) % Y, c))
Y_DOWN = tensor_pairs(lambda zh, y, c: (zh, (y - 1) % Y, c))
ROW_GROUPS = [[tensor_id(zh, y, c) for zh in range(Z_HI) for y in range(Y)] for c in range(CORE)]


def seq_pairs(dx, dz):
    return [(x * Z_LO + z, (x ^ dx) * Z_LO + (z ^ dz)) for x in range(X) for z in range(Z_LO)]


X_EVEN = seq_pairs(1, 0)
X_ODD = seq_pairs(3, 0)
Z_TRADE = [seq_pairs(0, r) for r in range(Z_LO)]

NT = (((1,), (1,)), ((), ()))


UP_PLACE = (4, 1, 0, 5)
DOWN_PLACE = (6, 7, 2, 3)


def columns(rows, index_ref, j, k, block):
    side_by_side = []
    for slot in (k, k + 1):
        at = pl.multiple_of(index_ref[j, slot] * block, block)
        side_by_side.append(rows[:, pl.ds(at, block)])
    return jnp.concatenate(side_by_side, axis=1)


def block_kernel(factor, place_ref, upi_ref, downi_ref, mine_a, mine_b, other_a, other_b, up_hbm, down_hbm,
                 send_ref, keep_ref, even_out, odd_out, up0, up3, down0, down1,
                 parts_ref, inputs, grads, acc_ref, up_ref, down_ref, pre_ref, pg_ref, act_ref, us_ref, ds_ref, sems, out_sem):
    hidden, slots, block, _ = up_ref.shape
    pieces, rows, quarter = keep_ref.shape
    share = up0.shape[2]

    split = mine_a.shape[0]

    def row_copies(parts, into, at):
        return [pltpu.make_async_copy(parts[0], into.at[0:split], sems.at[at, 0]),
                pltpu.make_async_copy(parts[1], into.at[split:], sems.at[at, 1])]

    def start_rows(into, at, wanted):
        @pl.when(place_ref[0] == wanted)
        def _():
            for load in row_copies((mine_a, mine_b), into, at):
                load.start()

        @pl.when(place_ref[0] != wanted)
        def _():
            for load in row_copies((other_a, other_b), into, at):
                load.start()

    start_rows(inputs, 2, 0)
    up_loads = [pltpu.make_async_copy(up_hbm.at[j], up_ref.at[j], sems.at[0, j]) for j in range(hidden)]
    down_loads = [pltpu.make_async_copy(down_hbm.at[j], down_ref.at[j], sems.at[1, j]) for j in range(hidden)]
    for load in up_loads:
        load.start()
    start_rows(grads, 3, 1)
    for load in down_loads:
        load.start()
    acc_ref[...] = jnp.zeros_like(acc_ref)
    for load in row_copies((mine_a, mine_b), inputs, 2):
        load.wait()
    for j in range(hidden):
        up_loads[j].wait()
        preact = 0.0
        for k in range(0, slots, 2):
            weights = up_ref[j, k:k + 2].reshape(2 * block, block)
            preact = preact + jnp.dot(columns(inputs, upi_ref, j, k, block), weights,
                                      preferred_element_type=jnp.float32)
        pre_ref[j] = preact
    for load in row_copies((mine_a, mine_b), grads, 3):
        load.wait()

    for j in range(hidden):
        down_loads[j].wait()
        preact, hidden_grad = pre_ref[j], 0.0
        for k in range(0, slots, 2):
            weights = jnp.concatenate([down_ref[j, k], down_ref[j, k + 1]], axis=1)
            hidden_grad = hidden_grad + lax.dot_general(
                columns(grads, downi_ref, j, k, block), weights, NT, preferred_element_type=jnp.float32)
        gating = jax.nn.sigmoid(preact)
        act_ref[j] = (preact * gating).astype(jnp.bfloat16).T
        pg = (hidden_grad * gating * (1.0 + preact * (1.0 - gating))).astype(jnp.bfloat16)
        pg_ref[j] = pg.T
        for k in range(0, slots, 2):
            terms = lax.dot_general(pg, up_ref[j, k:k + 2].reshape(2 * block, block), NT,
                                    preferred_element_type=jnp.float32)
            for slot in (k, k + 1):
                at = pl.multiple_of(upi_ref[j, slot] * block, block)
                acc_ref[:, pl.ds(at, block)] += terms[:, (slot - k) * block:(slot - k + 1) * block]

    stores = []

    def store(first, last, at):
        here = pl.ds(first, last - first)
        pairs = [(parts_ref.at[0:2, here], even_out.at[:, here]), (parts_ref.at[2:4, here], odd_out.at[:, here])]
        pairs += [(parts_ref.at[4 + n, here], out.at[here]) for n, out in enumerate((up0, up3, down0, down1))]
        for n, pair in enumerate(pairs):
            stores.append(pltpu.make_async_copy(*pair, out_sem.at[at, n]))
            stores[-1].start()

    for j in range(hidden):
        pg = pg_ref[j]
        act = act_ref[j]
        for k in range(0, slots, 2):
            sums = jnp.dot(pg, columns(inputs, upi_ref, j, k, block), preferred_element_type=jnp.float32)
            sums = (sums * factor).astype(jnp.bfloat16)
            for slot in (k, k + 1):
                us_ref[slot] = sums[:, (slot - k) * block:(slot - k + 1) * block].T
            sums = jnp.dot(act, columns(grads, downi_ref, j, k, block), preferred_element_type=jnp.float32)
            sums = (sums * factor).astype(jnp.bfloat16)
            for slot in (k, k + 1):
                ds_ref[slot] = sums[:, (slot - k) * block:(slot - k + 1) * block]
        for q in range(X):
            row = pl.multiple_of((place_ref[1] ^ q) * share, share)
            parts_ref[UP_PLACE[q], j] = us_ref[:, pl.ds(row, share), :]
            parts_ref[DOWN_PLACE[q], j] = ds_ref[:, pl.ds(row, share), :]
        if j == hidden // 2:
            store(0, j + 1, 0)
    store(hidden // 2 + 1, hidden, 1)

    z_hi = place_ref[4]
    for out, core in ((send_ref, 1 - place_ref[0]), (keep_ref, place_ref[0])):
        left = pl.multiple_of(core * 2 * quarter, quarter)
        right = pl.multiple_of(core * 2 * quarter + quarter, quarter)
        for at, k in enumerate(FIRST + SECOND):
            owner = (place_ref[3] - k) & (Y - 1)
            here = slice(at * rows, (at + 1) * rows)
            a = acc_ref[here, pl.ds(left, quarter)]
            b = acc_ref[here, pl.ds(right, quarter)]
            half = rows // 2
            out[z_hi * Y + owner] = jnp.concatenate([a[:half], b[:half]], axis=0).astype(jnp.bfloat16)
            out[(1 - z_hi) * Y + owner] = jnp.concatenate([a[half:], b[half:]], axis=0).astype(jnp.bfloat16)
    for copy in stores:
        copy.wait()


def x_sum_kernel(place_ref, up_own, up_a, up_b, down_own, down_a, down_b, *refs):
    outs, sum_ref = refs[:Z_LO], refs[Z_LO]
    hidden, slots, share, block = up_own.shape
    rows = share // Z_LO
    for kind, parts in enumerate(((up_own, up_a.at[1], up_b), (down_own, down_a, down_b.at[1]))):
        for j in range(hidden):
            total = sum(part[j].astype(jnp.float32) for part in parts)
            sum_ref[kind, j] = total.reshape(slots * share, block)
            for r, out in enumerate(outs):
                row = pl.multiple_of((place_ref[2] ^ r) * rows, rows)
                piece = [sum_ref[kind, j, pl.ds(k * share + row, rows), :] for k in range(slots)]
                out[kind, j] = jnp.concatenate(piece, axis=0).astype(jnp.bfloat16)


def add_kernel(a_ref, b_ref, out_ref):
    out_ref[...] = (a_ref[...].astype(jnp.float32) + b_ref[...].astype(jnp.float32)).astype(jnp.bfloat16)


def total_kernel(parts_ref, out_ref):
    total = sum(parts_ref[n].astype(jnp.float32) for n in range(parts_ref.shape[0]))
    out_ref[...] = total.astype(jnp.bfloat16)


SMEM = pl.BlockSpec(memory_space=pltpu.SMEM)
VMEM = pl.BlockSpec(memory_space=pltpu.VMEM)
HBM = pl.BlockSpec(memory_space=pltpu.HBM)


def block_parts(factor, place, up_index, down_index, gathered, up_blocks, down_blocks):
    hidden, slots, block, _ = up_blocks.shape
    rows = gathered[0].shape[0] + gathered[1].shape[0]
    features = gathered[0].shape[1]
    flops = 5 * 2 * rows * hidden * slots * block * block
    terms = jax.ShapeDtypeStruct((Z_HI * Y, rows // Y, features // 4), jnp.bfloat16)
    part = jax.ShapeDtypeStruct((hidden, slots, block // X, block), jnp.bfloat16)
    both = jax.ShapeDtypeStruct((2,) + part.shape, jnp.bfloat16)
    return pl.pallas_call(
        functools.partial(block_kernel, factor),
        in_specs=[SMEM] * 3 + [HBM] * 6,
        out_specs=[VMEM] * 2 + [HBM] * 6,
        out_shape=[terms] * 2 + [both] * 2 + [part] * 4,
        scratch_shapes=[
            pltpu.VMEM((2 * X,) + part.shape, jnp.bfloat16),
            pltpu.VMEM((rows, features), jnp.bfloat16),
            pltpu.VMEM((rows, features), jnp.bfloat16),
            pltpu.VMEM((rows, features), jnp.float32),
            pltpu.VMEM(up_blocks.shape, jnp.bfloat16),
            pltpu.VMEM(down_blocks.shape, jnp.bfloat16),
            pltpu.VMEM((hidden, rows, block), jnp.float32),
            pltpu.VMEM((hidden, block, rows), jnp.bfloat16),
            pltpu.VMEM((hidden, block, rows), jnp.bfloat16),
            pltpu.VMEM((slots, block, block), jnp.bfloat16),
            pltpu.VMEM((slots, block, block), jnp.bfloat16),
            pltpu.SemaphoreType.DMA((4, hidden)),
            pltpu.SemaphoreType.DMA((2, 6)),
        ],
        compiler_params=pltpu.CompilerParams(vmem_limit_bytes=58 * 2**20),
        cost_estimate=pl.CostEstimate(flops=flops, bytes_accessed=16 * 2**20, transcendentals=0),
        name="block_parts",
    )(place, up_index, down_index, *gathered, up_blocks, down_blocks)


def x_sum(place, *parts):
    hidden, slots, share, block = parts[0].shape
    rows = slots * share // Z_LO
    return pl.pallas_call(
        x_sum_kernel,
        in_specs=[SMEM] + [VMEM] * 6,
        out_specs=[VMEM] * Z_LO,
        out_shape=[jax.ShapeDtypeStruct((2, hidden, rows, block), jnp.bfloat16)] * Z_LO,
        scratch_shapes=[pltpu.VMEM((2, hidden, slots * share, block), jnp.float32)],
        compiler_params=pltpu.CompilerParams(vmem_limit_bytes=8 * 2**20),
        cost_estimate=pl.CostEstimate(flops=2**21, bytes_accessed=4 * 2**20, transcendentals=0),
        name="x_sum",
    )(place, *parts)


def cost(microseconds):
    return pl.CostEstimate(flops=microseconds * 10**9, bytes_accessed=2**20, transcendentals=0)


SMALL = pltpu.CompilerParams(vmem_limit_bytes=6 * 2**20)


def add_terms(a, b, microseconds, name):
    half = a.shape[0] // 2 if a.shape[0] % 2 == 0 else a.shape[0]
    rest = (0,) * (a.ndim - 1)
    spec = pl.BlockSpec((half,) + a.shape[1:], lambda i: (i,) + rest)
    first = pl.BlockSpec((None, half) + a.shape[1:], lambda i: (0, i) + rest)
    return pl.pallas_call(
        add_kernel, grid=(a.shape[0] // half,), in_specs=[spec, first if b.ndim > a.ndim else spec], out_specs=spec,
        out_shape=jax.ShapeDtypeStruct(a.shape, jnp.bfloat16), cost_estimate=cost(microseconds), name=name,
        compiler_params=SMALL,
    )(a, b)


def total_terms(parts):
    pieces, rows, width = parts.shape
    share = width // 4
    return pl.pallas_call(
        total_kernel, grid=(4,),
        in_specs=[pl.BlockSpec((pieces, rows, share), lambda i: (0, 0, i))],
        out_specs=pl.BlockSpec((rows, share), lambda i: (0, i)),
        out_shape=jax.ShapeDtypeStruct((rows, width), jnp.bfloat16), cost_estimate=cost(30), name="total_terms", compiler_params=SMALL,
    )(parts)


def in_order(first_is_mine, mine, other):
    a = jnp.where(first_is_mine, mine, other)
    b = jnp.where(first_is_mine, other, mine)
    return jnp.concatenate([a, b], axis=0)


FIRST = (0, 1, 7, 2, 6, 3)
SECOND = (5, 4)


def gather_rows(inputs, grad_out, core, zero):
    send = jnp.where(core == 0, grad_out, inputs)
    keep = jnp.where(core == 0, inputs, grad_out)
    pair = in_order(core == 0, keep, lax.ppermute(send, "tensor", SIBLING))
    rows, features = pair.shape
    half = features // 2
    pair = jnp.concatenate([pair[:, :half], pair[:, half:]], axis=0)
    other = lax.ppermute(pair, "tensor", Z_PARTNER)
    left = jnp.concatenate([pair[:rows], other[:rows]], axis=0)
    right = jnp.concatenate([pair[rows:], other[rows:]], axis=0)
    chunk = lax.optimization_barrier(jnp.concatenate([left, right], axis=1))
    first = jnp.zeros((len(FIRST), 2 * rows, features), chunk.dtype)
    second = jnp.zeros((len(SECOND), 2 * rows, features), chunk.dtype)

    def place(whole, piece, at, column=0):
        return lax.dynamic_update_slice(whole, piece[None], (zero + at, 0, column))

    first = place(first, chunk, FIRST.index(0))
    up = down = chunk
    for step in range(1, Y // 2):
        up = lax.ppermute(up, "tensor", Y_UP)
        down = lax.ppermute(down, "tensor", Y_DOWN)
        first = place(first, up, FIRST.index(step))
        if Y - step in FIRST:
            first = place(first, down, FIRST.index(Y - step))
    second = place(second, down, SECOND.index(Y // 2 + 1))
    second = place(second, lax.ppermute(up[:, :half], "tensor", Y_UP), SECOND.index(Y // 2))
    second = place(second, lax.ppermute(down[:, half:], "tensor", Y_DOWN), SECOND.index(Y // 2), half)
    return first.reshape(-1, features), second.reshape(-1, features)


def reduce_weights_x(place, even, odd, up_own, up_odd, down_own, down_even):
    even = lax.ppermute(even, "seq", X_EVEN)
    odd = lax.ppermute(odd, "seq", X_ODD)
    up_odd = lax.ppermute(add_terms(up_odd, even, 20, "add_up"), "seq", X_ODD)
    down_even = lax.ppermute(add_terms(down_even, odd, 20, "add_down"), "seq", X_EVEN)
    return x_sum(place, up_own, even, up_odd, down_own, down_even, odd)


def reduce_inputs(keep, send):
    part = add_terms(keep, lax.ppermute(send, "tensor", SIBLING), 15, "add_cores")
    return lax.all_to_all(part, "tensor", 0, 0, axis_index_groups=ROW_GROUPS, tiled=True)


def own_rows(part, core):
    part = total_terms(part)
    rows = part.shape[0] // 4
    pair = jnp.concatenate([part[:2 * rows], part[2 * rows:]], axis=1)
    mine = jnp.where(core == 0, pair[:rows], pair[rows:])
    other = lax.ppermute(jnp.where(core == 0, pair[rows:], pair[:rows]), "tensor", SIBLING)
    left = jnp.where(core == 0, mine, other)
    right = jnp.where(core == 0, other, mine)
    return jnp.concatenate([left, right], axis=1)


def local(inputs, grad_out, up_blocks, up_index, down_blocks, down_index):
    t = lax.axis_index("tensor")
    core = t & (CORE - 1)
    z_hi = t >> 4
    rows_here, _ = inputs.shape
    factor = 1.0 / math.sqrt(rows_here * lax.axis_size("tensor") * lax.axis_size("seq"))
    first, second = gather_rows(inputs, grad_out, core, t >> 5)
    gathered = (first, second, lax.ppermute(first, "tensor", SIBLING), lax.ppermute(second, "tensor", SIBLING))
    seq = lax.axis_index("seq")
    y = (t >> 1) & (Y - 1)
    place = jnp.stack([core, seq >> 2, seq & (Z_LO - 1), y, z_hi]).astype(jnp.int32)
    send, keep, *parts = block_parts(factor, place, up_index, down_index, gathered, up_blocks, down_blocks)
    hidden, slots, block, _ = up_blocks.shape
    shape = (hidden, slots, block // (X * Z_LO), block)
    input_terms = reduce_inputs(keep, send)
    pieces = reduce_weights_x(place, *parts)
    first = pieces[0]
    input_terms, first = lax.optimization_barrier((input_terms, first))
    grad_in = own_rows(input_terms, core)
    pieces = [first] + [lax.ppermute(pieces[r], "seq", Z_TRADE[r]) for r in (2, 3, 1)]
    total = sum(piece.astype(jnp.float32) for piece in pieces).astype(jnp.bfloat16)
    grad_up, grad_down = total[0].reshape(shape), total[1].reshape(shape)
    return (grad_in, grad_up, grad_down)


def solution(mesh):
    return jax.shard_map(
        local,
        mesh=mesh,
        in_specs=(
            P(("seq", "tensor"), None),
            P(("seq", "tensor"), None),
            P("tensor", None, None, None),
            P("tensor", None),
            P("tensor", None, None, None),
            P("tensor", None),
        ),
        out_specs=(
            P(("seq", "tensor"), None),
            P("tensor", None, "seq", None),
            P("tensor", None, "seq", None),
        ),
        check_vma=False,
    )
```

```python
import functools
import math

import jax
import jax.numpy as jnp
from jax import lax
from jax.experimental import pallas as pl
from jax.experimental.pallas import tpu as pltpu
from jax.sharding import PartitionSpec as P

Z_HI, Y, CORE = 2, 8, 2
X, Z_LO = 4, 4


def tensor_id(zh, y, c):
    return (zh * Y + y) * CORE + c


def tensor_pairs(move):
    return [
        (tensor_id(zh, y, c), tensor_id(*move(zh, y, c)))
        for zh in range(Z_HI)
        for y in range(Y)
        for c in range(CORE)
    ]


SIBLING = tensor_pairs(lambda zh, y, c: (zh, y, 1 - c))
Z_PARTNER = tensor_pairs(lambda zh, y, c: (1 - zh, y, c))
Y_UP = tensor_pairs(lambda zh, y, c: (zh, (y + 1) % Y, c))
Y_DOWN = tensor_pairs(lambda zh, y, c: (zh, (y - 1) % Y, c))
ROW_GROUPS = [[tensor_id(zh, y, c) for zh in range(Z_HI) for y in range(Y)] for c in range(CORE)]


def seq_pairs(dx, dz):
    return [(x * Z_LO + z, (x ^ dx) * Z_LO + (z ^ dz)) for x in range(X) for z in range(Z_LO)]


X_EVEN = seq_pairs(1, 0)
X_ODD = seq_pairs(3, 0)
Z_TRADE = [seq_pairs(0, r) for r in range(Z_LO)]

NT = (((1,), (1,)), ((), ()))


UP_PLACE = (4, 1, 0, 5)
DOWN_PLACE = (6, 7, 2, 3)


def columns(rows, index_ref, j, k, block):
    side_by_side = []
    for slot in (k, k + 1):
        at = pl.multiple_of(index_ref[j, slot] * block, block)
        side_by_side.append(rows[:, pl.ds(at, block)])
    return jnp.concatenate(side_by_side, axis=1)


def block_kernel(factor, place_ref, upi_ref, downi_ref, mine_a, mine_b, other_a, other_b, up_hbm, down_hbm,
                 send_ref, keep_ref, even_out, odd_out, up0, up3, down0, down1,
                 parts_ref, inputs, grads, acc_ref, up_ref, down_ref, pre_ref, pg_ref, act_ref, us_ref, ds_ref, sems, out_sem):
    hidden, slots, block, _ = up_ref.shape
    pieces, rows, quarter = keep_ref.shape
    share = up0.shape[2]

    split = mine_a.shape[0]

    def row_copies(parts, into, at):
        return [pltpu.make_async_copy(parts[0], into.at[0:split], sems.at[at, 0]),
                pltpu.make_async_copy(parts[1], into.at[split:], sems.at[at, 1])]

    def start_rows(into, at, wanted):
        @pl.when(place_ref[0] == wanted)
        def _():
            for load in row_copies((mine_a, mine_b), into, at):
                load.start()

        @pl.when(place_ref[0] != wanted)
        def _():
            for load in row_copies((other_a, other_b), into, at):
                load.start()

    start_rows(inputs, 2, 0)
    up_loads = [pltpu.make_async_copy(up_hbm.at[j], up_ref.at[j], sems.at[0, j]) for j in range(hidden)]
    down_loads = [pltpu.make_async_copy(down_hbm.at[j], down_ref.at[j], sems.at[1, j]) for j in range(hidden)]
    for load in up_loads:
        load.start()
    start_rows(grads, 3, 1)
    for load in down_loads:
        load.start()
    acc_ref[...] = jnp.zeros_like(acc_ref)
    for load in row_copies((mine_a, mine_b), inputs, 2):
        load.wait()
    for j in range(hidden):
        up_loads[j].wait()
        preact = 0.0
        for k in range(0, slots, 2):
            weights = up_ref[j, k:k + 2].reshape(2 * block, block)
            preact = preact + jnp.dot(columns(inputs, upi_ref, j, k, block), weights,
                                      preferred_element_type=jnp.float32)
        pre_ref[j] = preact
    for load in row_copies((mine_a, mine_b), grads, 3):
        load.wait()

    for j in range(hidden):
        down_loads[j].wait()
        preact, hidden_grad = pre_ref[j], 0.0
        for k in range(0, slots, 2):
            weights = jnp.concatenate([down_ref[j, k], down_ref[j, k + 1]], axis=1)
            hidden_grad = hidden_grad + lax.dot_general(
                columns(grads, downi_ref, j, k, block), weights, NT, preferred_element_type=jnp.float32)
        gating = jax.nn.sigmoid(preact)
        act_ref[j] = (preact * gating).astype(jnp.bfloat16).T
        pg = (hidden_grad * gating * (1.0 + preact * (1.0 - gating))).astype(jnp.bfloat16)
        pg_ref[j] = pg.T
        for k in range(0, slots, 2):
            terms = lax.dot_general(pg, up_ref[j, k:k + 2].reshape(2 * block, block), NT,
                                    preferred_element_type=jnp.float32)
            for slot in (k, k + 1):
                at = pl.multiple_of(upi_ref[j, slot] * block, block)
                acc_ref[:, pl.ds(at, block)] += terms[:, (slot - k) * block:(slot - k + 1) * block]

    stores = []

    def store(first, last, at):
        here = pl.ds(first, last - first)
        pairs = [(parts_ref.at[0:2, here], even_out.at[:, here]), (parts_ref.at[2:4, here], odd_out.at[:, here])]
        pairs += [(parts_ref.at[4 + n, here], out.at[here]) for n, out in enumerate((up0, up3, down0, down1))]
        for n, pair in enumerate(pairs):
            stores.append(pltpu.make_async_copy(*pair, out_sem.at[at, n]))
            stores[-1].start()

    for j in range(hidden):
        pg = pg_ref[j]
        act = act_ref[j]
        for k in range(0, slots, 2):
            sums = jnp.dot(pg, columns(inputs, upi_ref, j, k, block), preferred_element_type=jnp.float32)
            sums = (sums * factor).astype(jnp.bfloat16)
            for slot in (k, k + 1):
                us_ref[slot] = sums[:, (slot - k) * block:(slot - k + 1) * block].T
            sums = jnp.dot(act, columns(grads, downi_ref, j, k, block), preferred_element_type=jnp.float32)
            sums = (sums * factor).astype(jnp.bfloat16)
            for slot in (k, k + 1):
                ds_ref[slot] = sums[:, (slot - k) * block:(slot - k + 1) * block]
        for q in range(X):
            row = pl.multiple_of((place_ref[1] ^ q) * share, share)
            parts_ref[UP_PLACE[q], j] = us_ref[:, pl.ds(row, share), :]
            parts_ref[DOWN_PLACE[q], j] = ds_ref[:, pl.ds(row, share), :]
        if j == hidden // 2:
            store(0, j + 1, 0)
    store(hidden // 2 + 1, hidden, 1)

    z_hi = place_ref[4]
    for out, core in ((send_ref, 1 - place_ref[0]), (keep_ref, place_ref[0])):
        left = pl.multiple_of(core * 2 * quarter, quarter)
        right = pl.multiple_of(core * 2 * quarter + quarter, quarter)
        for at, k in enumerate(FIRST + SECOND):
            owner = (place_ref[3] - k) & (Y - 1)
            here = slice(at * rows, (at + 1) * rows)
            a = acc_ref[here, pl.ds(left, quarter)]
            b = acc_ref[here, pl.ds(right, quarter)]
            half = rows // 2
            out[z_hi * Y + owner] = jnp.concatenate([a[:half], b[:half]], axis=0).astype(jnp.bfloat16)
            out[(1 - z_hi) * Y + owner] = jnp.concatenate([a[half:], b[half:]], axis=0).astype(jnp.bfloat16)
    for copy in stores:
        copy.wait()


def x_sum_kernel(place_ref, up_own, up_a, up_b, down_own, down_a, down_b, *refs):
    outs, sum_ref = refs[:Z_LO], refs[Z_LO]
    hidden, slots, share, block = up_own.shape
    rows = share // Z_LO
    for kind, parts in enumerate(((up_own, up_a.at[1], up_b), (down_own, down_a, down_b.at[1]))):
        for j in range(hidden):
            total = sum(part[j].astype(jnp.float32) for part in parts)
            sum_ref[kind, j] = total.reshape(slots * share, block)
            for r, out in enumerate(outs):
                row = pl.multiple_of((place_ref[2] ^ r) * rows, rows)
                piece = [sum_ref[kind, j, pl.ds(k * share + row, rows), :] for k in range(slots)]
                out[kind, j] = jnp.concatenate(piece, axis=0).astype(jnp.bfloat16)


def add_kernel(a_ref, b_ref, out_ref):
    out_ref[...] = (a_ref[...].astype(jnp.float32) + b_ref[...].astype(jnp.float32)).astype(jnp.bfloat16)


def total_kernel(parts_ref, out_ref):
    total = sum(parts_ref[n].astype(jnp.float32) for n in range(parts_ref.shape[0]))
    out_ref[...] = total.astype(jnp.bfloat16)


SMEM = pl.BlockSpec(memory_space=pltpu.SMEM)
VMEM = pl.BlockSpec(memory_space=pltpu.VMEM)
HBM = pl.BlockSpec(memory_space=pltpu.HBM)


def block_parts(factor, place, up_index, down_index, gathered, up_blocks, down_blocks):
    hidden, slots, block, _ = up_blocks.shape
    rows = gathered[0].shape[0] + gathered[1].shape[0]
    features = gathered[0].shape[1]
    flops = 5 * 2 * rows * hidden * slots * block * block
    terms = jax.ShapeDtypeStruct((Z_HI * Y, rows // Y, features // 4), jnp.bfloat16)
    part = jax.ShapeDtypeStruct((hidden, slots, block // X, block), jnp.bfloat16)
    both = jax.ShapeDtypeStruct((2,) + part.shape, jnp.bfloat16)
    return pl.pallas_call(
        functools.partial(block_kernel, factor),
        in_specs=[SMEM] * 3 + [HBM] * 6,
        out_specs=[VMEM] * 2 + [HBM] * 6,
        out_shape=[terms] * 2 + [both] * 2 + [part] * 4,
        scratch_shapes=[
            pltpu.VMEM((2 * X,) + part.shape, jnp.bfloat16),
            pltpu.VMEM((rows, features), jnp.bfloat16),
            pltpu.VMEM((rows, features), jnp.bfloat16),
            pltpu.VMEM((rows, features), jnp.float32),
            pltpu.VMEM(up_blocks.shape, jnp.bfloat16),
            pltpu.VMEM(down_blocks.shape, jnp.bfloat16),
            pltpu.VMEM((hidden, rows, block), jnp.float32),
            pltpu.VMEM((hidden, block, rows), jnp.bfloat16),
            pltpu.VMEM((hidden, block, rows), jnp.bfloat16),
            pltpu.VMEM((slots, block, block), jnp.bfloat16),
            pltpu.VMEM((slots, block, block), jnp.bfloat16),
            pltpu.SemaphoreType.DMA((4, hidden)),
            pltpu.SemaphoreType.DMA((2, 6)),
        ],
        compiler_params=pltpu.CompilerParams(vmem_limit_bytes=58 * 2**20),
        cost_estimate=pl.CostEstimate(flops=flops, bytes_accessed=16 * 2**20, transcendentals=0),
        name="block_parts",
    )(place, up_index, down_index, *gathered, up_blocks, down_blocks)


def x_sum(place, *parts):
    hidden, slots, share, block = parts[0].shape
    rows = slots * share // Z_LO
    return pl.pallas_call(
        x_sum_kernel,
        in_specs=[SMEM] + [VMEM] * 6,
        out_specs=[VMEM] * Z_LO,
        out_shape=[jax.ShapeDtypeStruct((2, hidden, rows, block), jnp.bfloat16)] * Z_LO,
        scratch_shapes=[pltpu.VMEM((2, hidden, slots * share, block), jnp.float32)],
        compiler_params=pltpu.CompilerParams(vmem_limit_bytes=8 * 2**20),
        cost_estimate=pl.CostEstimate(flops=2**21, bytes_accessed=4 * 2**20, transcendentals=0),
        name="x_sum",
    )(place, *parts)


def cost(microseconds):
    return pl.CostEstimate(flops=microseconds * 10**9, bytes_accessed=2**20, transcendentals=0)


SMALL = pltpu.CompilerParams(vmem_limit_bytes=6 * 2**20)


def add_terms(a, b, microseconds, name):
    half = a.shape[0] // 2 if a.shape[0] % 2 == 0 else a.shape[0]
    rest = (0,) * (a.ndim - 1)
    spec = pl.BlockSpec((half,) + a.shape[1:], lambda i: (i,) + rest)
    first = pl.BlockSpec((None, half) + a.shape[1:], lambda i: (0, i) + rest)
    return pl.pallas_call(
        add_kernel, grid=(a.shape[0] // half,), in_specs=[spec, first if b.ndim > a.ndim else spec], out_specs=spec,
        out_shape=jax.ShapeDtypeStruct(a.shape, jnp.bfloat16), cost_estimate=cost(microseconds), name=name,
        compiler_params=SMALL,
    )(a, b)


def total_terms(parts):
    pieces, rows, width = parts.shape
    share = width // 4
    return pl.pallas_call(
        total_kernel, grid=(4,),
        in_specs=[pl.BlockSpec((pieces, rows, share), lambda i: (0, 0, i))],
        out_specs=pl.BlockSpec((rows, share), lambda i: (0, i)),
        out_shape=jax.ShapeDtypeStruct((rows, width), jnp.bfloat16), cost_estimate=cost(30), name="total_terms", compiler_params=SMALL,
    )(parts)


def in_order(first_is_mine, mine, other):
    a = jnp.where(first_is_mine, mine, other)
    b = jnp.where(first_is_mine, other, mine)
    return jnp.concatenate([a, b], axis=0)


FIRST = (0, 1, 7, 2, 6, 3)
SECOND = (5, 4)


def gather_rows(inputs, grad_out, core, zero):
    send = jnp.where(core == 0, grad_out, inputs)
    keep = jnp.where(core == 0, inputs, grad_out)
    pair = in_order(core == 0, keep, lax.ppermute(send, "tensor", SIBLING))
    rows, features = pair.shape
    half = features // 2
    pair = jnp.concatenate([pair[:, :half], pair[:, half:]], axis=0)
    other = lax.ppermute(pair, "tensor", Z_PARTNER)
    left = jnp.concatenate([pair[:rows], other[:rows]], axis=0)
    right = jnp.concatenate([pair[rows:], other[rows:]], axis=0)
    chunk = lax.optimization_barrier(jnp.concatenate([left, right], axis=1))
    first = jnp.zeros((len(FIRST), 2 * rows, features), chunk.dtype)
    second = jnp.zeros((len(SECOND), 2 * rows, features), chunk.dtype)

    def place(whole, piece, at, column=0):
        return lax.dynamic_update_slice(whole, piece[None], (zero + at, 0, column))

    first = place(first, chunk, FIRST.index(0))
    up = down = chunk
    for step in range(1, Y // 2):
        up = lax.ppermute(up, "tensor", Y_UP)
        down = lax.ppermute(down, "tensor", Y_DOWN)
        first = place(first, up, FIRST.index(step))
        if Y - step in FIRST:
            first = place(first, down, FIRST.index(Y - step))
    second = place(second, down, SECOND.index(Y // 2 + 1))
    second = place(second, lax.ppermute(up[:, :half], "tensor", Y_UP), SECOND.index(Y // 2))
    second = place(second, lax.ppermute(down[:, half:], "tensor", Y_DOWN), SECOND.index(Y // 2), half)
    return first.reshape(-1, features), second.reshape(-1, features)


def reduce_weights_x(place, even, odd, up_own, up_odd, down_own, down_even):
    even = lax.ppermute(even, "seq", X_EVEN)
    odd = lax.ppermute(odd, "seq", X_ODD)
    up_odd = lax.ppermute(add_terms(up_odd, even, 20, "add_up"), "seq", X_ODD)
    down_even = lax.ppermute(add_terms(down_even, odd, 20, "add_down"), "seq", X_EVEN)
    return x_sum(place, up_own, even, up_odd, down_own, down_even, odd)


def reduce_inputs(keep, send):
    part = add_terms(keep, lax.ppermute(send, "tensor", SIBLING), 15, "add_cores")
    return lax.all_to_all(part, "tensor", 0, 0, axis_index_groups=ROW_GROUPS, tiled=True)


def own_rows(part, core):
    part = total_terms(part)
    rows = part.shape[0] // 4
    pair = jnp.concatenate([part[:2 * rows], part[2 * rows:]], axis=1)
    mine = jnp.where(core == 0, pair[:rows], pair[rows:])
    other = lax.ppermute(jnp.where(core == 0, pair[rows:], pair[:rows]), "tensor", SIBLING)
    left = jnp.where(core == 0, mine, other)
    right = jnp.where(core == 0, other, mine)
    return jnp.concatenate([left, right], axis=1)


def local(inputs, grad_out, up_blocks, up_index, down_blocks, down_index):
    t = lax.axis_index("tensor")
    core = t & (CORE - 1)
    z_hi = t >> 4
    rows_here, _ = inputs.shape
    factor = 1.0 / math.sqrt(rows_here * lax.axis_size("tensor") * lax.axis_size("seq"))
    first, second = gather_rows(inputs, grad_out, core, t >> 5)
    gathered = (first, second, lax.ppermute(first, "tensor", SIBLING), lax.ppermute(second, "tensor", SIBLING))
    seq = lax.axis_index("seq")
    y = (t >> 1) & (Y - 1)
    place = jnp.stack([core, seq >> 2, seq & (Z_LO - 1), y, z_hi]).astype(jnp.int32)
    send, keep, *parts = block_parts(factor, place, up_index, down_index, gathered, up_blocks, down_blocks)
    hidden, slots, block, _ = up_blocks.shape
    shape = (hidden, slots, block // (X * Z_LO), block)
    input_terms = reduce_inputs(keep, send)
    pieces = reduce_weights_x(place, *parts)
    first = pieces[0]
    input_terms, first = lax.optimization_barrier((input_terms, first))
    grad_in = own_rows(input_terms, core)
    pieces = [first] + [lax.ppermute(pieces[r], "seq", Z_TRADE[r]) for r in (3, 2, 1)]
    total = sum(piece.astype(jnp.float32) for piece in pieces).astype(jnp.bfloat16)
    grad_up, grad_down = total[0].reshape(shape), total[1].reshape(shape)
    return (grad_in, grad_up, grad_down)


def solution(mesh):
    return jax.shard_map(
        local,
        mesh=mesh,
        in_specs=(
            P(("seq", "tensor"), None),
            P(("seq", "tensor"), None),
            P("tensor", None, None, None),
            P("tensor", None),
            P("tensor", None, None, None),
            P("tensor", None),
        ),
        out_specs=(
            P(("seq", "tensor"), None),
            P("tensor", None, "seq", None),
            P("tensor", None, "seq", None),
        ),
        check_vma=False,
    )
```
